32 devices in a mesh: dp: 8 (over y, x, core), tensor: 4 (over z).
Axes of the slice: x: 2, y: 2, z: 4, core: 2. Of those that a mesh axis runs over, the one named last changes fastest.
Arguments:
- out_grad: bfloat16 [8, 256, 4096], P('dp', 'tensor'), may hold values from -6 to 6
- out_weight: bfloat16 [4096, 1024], P('dp', 'tensor'), may hold values from -0.1875 to 0.1875
- queries: bfloat16 [8, 256, 1024], P('dp', None, 'tensor'), may hold values from -5 to 5
- keys: bfloat16 [8, 256, 512], P('dp', None, 'tensor'), may hold values from -5 to 5, as said below
- values: bfloat16 [8, 256, 512], P('dp', None, 'tensor'), may hold values from -6 to 6, as said below
- segment_ids: int32 [8, 256], P('dp'), may hold values from 0 to 3, never falling along the last dimension, each value on 1 to 128 neighbouring positions
Outputs:
- d_queries: bfloat16 [8, 256, 1024], P('dp', None, 'tensor')
- d_keys: bfloat16 [8, 256, 512], P('dp', None, 'tensor')
- d_values: bfloat16 [8, 256, 512], P('dp', None, 'tensor')
- d_out_weight: float32 [4096, 1024], P('dp', 'tensor')
The draws below stay inside these ranges and needn't reach their ends.
Inputs may be any that keep to these rules, and one draw needn't show every extreme that they name: `keys`: column blocks 2 g and 2 g + 1 are equal. `values`: column blocks 2 g and 2 g + 1 are equal.
All inputs are finite; a program needn't handle non-finite values.
Results may differ from the reference program's by a relative error of at most 0.018.
Values may be sent and summed in bfloat16 or wider, within the bound.
A program may use at most 128 MiB of HBM per device.

```python
import math
import jax
import jax.numpy as jnp
import numpy as np
from jax import lax

D = 4096
HD = 128
DOCS = 4
HEADS = 8
KV_HEADS = 2
LEN = 256
SEQS = 8
DOC_MOST = 128


def draw_queries(key, part):
    group = HEADS // KV_HEADS
    base = jnp.clip(jax.random.normal(jax.random.fold_in(key, 1), (SEQS, LEN, KV_HEADS, group, HD), jnp.float32), -5.0, 5.0)
    return base.reshape(SEQS, LEN, HEADS * HD).astype(jnp.bfloat16)


def draw_keys(key, part):
    base = jnp.clip(jax.random.normal(jax.random.fold_in(key, 2), (SEQS, LEN, KV_HEADS, HD), jnp.float32), -5.0, 5.0)
    doubled = jnp.repeat(base[:, :, :, None, :], 2, axis=3)
    return doubled.reshape(SEQS, LEN, 2 * KV_HEADS * HD).astype(jnp.bfloat16)


def draw_values(key, part):
    base = jnp.clip(jax.random.normal(jax.random.fold_in(key, 3), (SEQS, LEN, KV_HEADS, HD), jnp.float32), -6.0, 6.0)
    doubled = jnp.repeat(base[:, :, :, None, :], 2, axis=3)
    return doubled.reshape(SEQS, LEN, 2 * KV_HEADS * HD).astype(jnp.bfloat16)


def raised(array, own_key, source, target, parts, factor):
    def block_of(dim):
        return (jnp.arange(array.shape[dim]) // (array.shape[dim] // parts)).reshape((-1,) + (1,) * (array.ndim - 1 - dim))

    first = jax.random.permutation(own_key, parts)[block_of(target)]
    other_side = (block_of(target) + parts // 2) % parts
    return jnp.where((block_of(source) == first) | (block_of(source) == other_side), factor * array, array)


def shard_levels(rng, shape, cuts, low, high):
    gain = 1.0
    for axis_at, shards_of in cuts:
        steps = jax.random.uniform(jax.random.fold_in(jax.random.fold_in(rng, 6), axis_at), (shards_of,), jnp.float32, low / len(cuts), high / len(cuts))
        gain = gain * jnp.repeat(jnp.exp(steps), shape[axis_at] // shards_of).reshape((-1,) + (1,) * (len(shape) - 1 - axis_at))
    return gain


def length_profile(amount, total, bound, skew):
    loads = [(1 << 20) // math.isqrt(rank ** skew) + 1 for rank in range(2, amount + 1)]
    rest, holding = total - bound - (amount - 1), [1] * (amount - 1)
    while rest > 0:
        free = [i for i in range(amount - 1) if holding[i] < bound]
        whole, remaining = sum([loads[i] for i in free]), rest
        for i in free:
            extra = min(bound - holding[i], max(1, remaining * loads[i] // whole), rest)
            holding[i] = holding[i] + extra
            rest = rest - extra
    return np.array([bound] + holding)


def ragged_sizes(own_key, number_of, total, limit, slope):
    if number_of == 2:
        one = jax.random.randint(own_key, (), max(1, total - limit), min(limit, total - 1) + 1)
        return jnp.stack([one, total - one])
    tallies = jnp.asarray(length_profile(number_of, total, limit, slope), jnp.int32)
    couples = (number_of - 1) // 2
    source_of, sink = tallies[1:1 + 2 * couples:2], tallies[2:2 + 2 * couples:2]
    margin = jnp.minimum(source_of - 1, limit - sink)
    moved = jax.random.randint(jax.random.fold_in(own_key, 1), (couples,), 0, 1 << 20) % (margin + 1)
    tallies = tallies.at[1:1 + 2 * couples:2].set(source_of - moved).at[2:2 + 2 * couples:2].set(sink + moved)
    return tallies[jax.random.permutation(jax.random.fold_in(own_key, 2), number_of)]


def noise(key, dims, width, bound, split=(), kind=jnp.bfloat16):
    drawn = jax.random.normal(key, dims, jnp.float32) * width
    if len(split) > 0:
        drawn = shard_levels(key, dims, split, -0.22, 0.18) * drawn
    return jnp.clip(drawn, min=-bound, max=bound).astype(kind)


def gaussian_with(rng, shape, width, most, shards, heavy, dtype=jnp.bfloat16):
    result = width * jax.random.normal(rng, shape, jnp.float32)
    if shards:
        result = result * shard_levels(rng, shape, shards, -0.22, 0.18)
    return jnp.clip(raised(result, jax.random.fold_in(rng, 3), *heavy), -most, most).astype(dtype)


def setup_inputs(seed: int = 0) -> dict:
    arg_keys = jax.random.split(jax.random.key(seed), 7)
    return {
        "out_grad": gaussian_with(arg_keys[0], (SEQS, LEN, D), 1.0, 6.0, ((0, 8), (1, 4)), (0, 2, 8, 2.0)),
        "out_weight": noise(arg_keys[1], (D, HEADS * HD), (HEADS * HD) ** -0.5, 0.1875, ((0, 8), (1, 4))),
        "queries": draw_queries(jax.random.fold_in(arg_keys[6], 71), 0),
        "keys": draw_keys(jax.random.fold_in(arg_keys[6], 71), 0),
        "values": draw_values(jax.random.fold_in(arg_keys[6], 71), 0),
        "segment_ids": jax.vmap(lambda own: jnp.searchsorted(jnp.cumsum(ragged_sizes(own, DOCS, LEN, DOC_MOST, 2)), jnp.arange(LEN), side="right"))(jax.random.split(arg_keys[5], SEQS)).reshape((SEQS, LEN)).astype(jnp.int32),
    }


def softmax_parts(query_heads, key_heads, segments):
    scores = jnp.einsum('qgjd,kgd->gjqk', query_heads.astype(jnp.float32), key_heads.astype(jnp.float32)) * (HD ** -0.5)
    position = jnp.arange(LEN)
    visible = (segments[:, None] == segments[None, :]) & (position[:, None] >= position[None, :])
    masked = jnp.where(visible, scores, -jnp.inf)
    top_score = jnp.max(masked, axis=-1, keepdims=True)
    raw_exp = jnp.exp(masked - top_score)
    return raw_exp / jnp.sum(raw_exp, axis=-1, keepdims=True)


def reference(out_grad, out_weight, queries, keys, values, segment_ids):
    group = HEADS // KV_HEADS
    scale = HD ** -0.5

    def one_sequence(carry, inputs):
        grad_rows, query_rows, key_rows, value_rows, segments = inputs
        query_heads = query_rows.reshape(LEN, KV_HEADS, group, HD)
        key_heads = key_rows.reshape(LEN, KV_HEADS, 2, HD)[:, :, 0, :]
        value_heads = value_rows.reshape(LEN, KV_HEADS, 2, HD)[:, :, 0, :]
        attn_prob = softmax_parts(query_heads, key_heads, segments)
        prob_low = attn_prob.astype(jnp.bfloat16)
        attn_out = jnp.einsum('gjqk,kgd->qgjd', prob_low.astype(jnp.float32), value_heads.astype(jnp.float32)).astype(jnp.bfloat16)
        flat_out = attn_out.reshape(LEN, HEADS * HD)
        grad_attn = jnp.dot(grad_rows, out_weight, preferred_element_type=jnp.float32).astype(jnp.bfloat16)
        weight_part = jnp.dot(grad_rows.T, flat_out, preferred_element_type=jnp.float32).astype(jnp.bfloat16)
        grad_heads = grad_attn.reshape(LEN, KV_HEADS, group, HD).astype(jnp.float32)
        deltas = jnp.sum(grad_heads * attn_out.astype(jnp.float32), axis=-1)
        grad_values = jnp.einsum('gjqk,qgjd->kgd', prob_low.astype(jnp.float32), grad_heads)
        grad_prob = jnp.einsum('qgjd,kgd->gjqk', grad_heads, value_heads.astype(jnp.float32))
        grad_score = (attn_prob * (grad_prob - jnp.transpose(deltas, (1, 2, 0))[..., None]) * scale).astype(jnp.bfloat16)
        grad_queries = jnp.einsum('gjqk,kgd->qgjd', grad_score.astype(jnp.float32), key_heads.astype(jnp.float32)).astype(jnp.bfloat16)
        grad_keys = jnp.einsum('gjqk,qgjd->kgd', grad_score.astype(jnp.float32), query_heads.astype(jnp.float32))
        keys_doubled = jnp.repeat(grad_keys, 2, axis=1).reshape(LEN, 2 * KV_HEADS * HD).astype(jnp.bfloat16)
        values_doubled = jnp.repeat(grad_values, 2, axis=1).reshape(LEN, 2 * KV_HEADS * HD).astype(jnp.bfloat16)
        return carry + weight_part.astype(jnp.float32), (grad_queries.reshape(LEN, HEADS * HD), keys_doubled, values_doubled)

    initial = jnp.zeros((D, HEADS * HD), jnp.float32)
    total, outputs = lax.scan(one_sequence, initial, (out_grad, queries, keys, values, segment_ids))
    d_queries, d_keys, d_values = outputs
    return d_queries, d_keys, d_values, total / SEQS
```

```python
import functools

import jax
import jax.numpy as jnp
from jax import lax
from jax.experimental import pallas as pl
from jax.experimental.pallas import tpu as pltpu
from jax.sharding import PartitionSpec as P

HD = 128
MESH = pl.DeviceIdType.MESH
F32 = jnp.float32
BF16 = jnp.bfloat16
ROWS = 256


def dot(a, b, ca, cb):
    return lax.dot_general(a, b, (((ca,), (cb,)), ((), ())), preferred_element_type=F32)


def kernel(
    nchip, n, grad_ref, weight_ref, q_ref, k_ref, v_ref, seg_ref,
    dq_ref, dk_ref, dv_ref, dw_ref,
    og, wfull, prob, seg_col, attn, gsum, kv_send, kv_recv,
    xsend, xrecv, part, rs_send, rs_recv,
    fill_sem, wfill_sem, rsend_sem, rrecv_sem, lsend_sem, lrecv_sem,
    wsend_sem, wrecv_sem, wxsend_sem, wxrecv_sem,
    xsend_sem, xrecv_sem, rss_sem, rsr_sem, kvs_sem, kvr_sem,
):
    d = lax.axis_index("dp")
    t = lax.axis_index("tensor")
    chip, core = d // 2, d % 2
    sibling = (chip * 2 + 1 - core, t)
    partner = (d, t + 1 - 2 * (t % 2))
    length, width = q_ref.shape
    depth = weight_ref.shape[0]
    heads = width // HD
    scale = HD ** (-0.5)
    has_left, has_right = t > 0, t < n - 1

    def behind(p):
        return lax.rem(chip - 1 - p + 2 * nchip, nchip)

    def ahead(p):
        return lax.rem(chip + 1 + p, nchip)

    def fill(j):
        return pltpu.make_async_copy(
            grad_ref.at[:, pl.ds(j * 2 * depth, 2 * depth)], og.at[j, t], fill_sem.at[j]
        )

    def wfill():
        return pltpu.make_async_copy(weight_ref, wfull.at[chip, core], wfill_sem)

    def go_right(p, s):
        at = og.at[behind(p), lax.rem(t - s + 1 + n, n)]
        return pltpu.make_async_remote_copy(
            at, at, rsend_sem.at[p, s - 1], rrecv_sem.at[p, s - 1],
            device_id=(d, lax.rem(t + 1, n)), device_id_type=MESH)

    def from_left(p, s):
        at = og.at[behind(p), lax.rem(t - s + n, n)]
        return pltpu.make_async_remote_copy(
            at, at, rsend_sem.at[p, s - 1], rrecv_sem.at[p, s - 1],
            device_id=(d, lax.rem(t + 1, n)), device_id_type=MESH)

    def go_left(p, s):
        at = og.at[behind(p), lax.rem(t + s - 1, n)]
        return pltpu.make_async_remote_copy(
            at, at, lsend_sem.at[p, s - 1], lrecv_sem.at[p, s - 1],
            device_id=(d, lax.rem(t - 1 + n, n)), device_id_type=MESH)

    def from_right(p, s):
        at = og.at[behind(p), lax.rem(t + s, n)]
        return pltpu.make_async_remote_copy(
            at, at, lsend_sem.at[p, s - 1], lrecv_sem.at[p, s - 1],
            device_id=(d, lax.rem(t - 1 + n, n)), device_id_type=MESH)

    def w_out(p):
        at = wfull.at[chip, core]
        return pltpu.make_async_remote_copy(
            at, at, wsend_sem.at[p], wrecv_sem.at[p],
            device_id=(ahead(p) * 2 + core, t), device_id_type=MESH)

    def w_in(p):
        at = wfull.at[behind(p), core]
        return pltpu.make_async_remote_copy(
            at, at, wsend_sem.at[p], wrecv_sem.at[p],
            device_id=(ahead(p) * 2 + core, t), device_id_type=MESH)

    def w_across(p):
        at = wfull.at[behind(p), core]
        return pltpu.make_async_remote_copy(
            at, at, wxsend_sem.at[p], wxrecv_sem.at[p], device_id=sibling, device_id_type=MESH)

    def w_from_sibling(p):
        at = wfull.at[behind(p), 1 - core]
        return pltpu.make_async_remote_copy(
            at, at, wxsend_sem.at[p], wxrecv_sem.at[p], device_id=sibling, device_id_type=MESH)

    def x_copy(p):
        return pltpu.make_async_remote_copy(
            xsend.at[p], xrecv.at[p], xsend_sem.at[p], xrecv_sem.at[p],
            device_id=sibling, device_id_type=MESH)

    def rs_copy(p):
        return pltpu.make_async_remote_copy(
            rs_send.at[p], rs_recv.at[p], rss_sem.at[p], rsr_sem.at[p],
            device_id=(behind(p) * 2 + core, t), device_id_type=MESH)

    def kv_copy():
        return pltpu.make_async_remote_copy(
            kv_send, kv_recv, kvs_sem, kvr_sem, device_id=partner, device_id_type=MESH)

    def send_own(p):
        @pl.when(has_right)
        def _():
            go_right(p, 1).start()

        @pl.when(has_left)
        def _():
            go_left(p, 1).start()

    for j in range(nchip):
        fill(j).start()
    wfill().start()

    barrier = pltpu.get_barrier_semaphore()

    @pl.when(has_left)
    def _():
        pl.semaphore_signal(barrier, 1, device_id=(d, lax.rem(t - 1 + n, n)), device_id_type=MESH)

    @pl.when(has_right)
    def _():
        pl.semaphore_signal(barrier, 1, device_id=(d, lax.rem(t + 1, n)), device_id_type=MESH)

    pl.semaphore_signal(barrier, 1, device_id=sibling, device_id_type=MESH)
    for p in range(nchip - 1):
        pl.semaphore_signal(barrier, 1, device_id=(ahead(p) * 2 + core, t), device_id_type=MESH)
    inner = has_left & has_right

    @pl.when(inner)
    def _():
        pl.semaphore_wait(barrier, nchip + 2)

    @pl.when(jnp.logical_not(inner))
    def _():
        pl.semaphore_wait(barrier, nchip + 1)

    for j in range(nchip):
        fill(j).wait()
    wfill().wait()
    send_own(0)
    for p in range(nchip - 1):
        w_out(p).start()
    w_across(nchip - 1).start()

    seg_col[...] = jnp.transpose(jnp.broadcast_to(seg_ref[...], (128, length)))
    rows = min(ROWS, length)
    blocks = length // rows

    def row_block(b):
        return pl.ds(pl.multiple_of(b * rows, rows), rows)

    def forward(b, carry):
        at = row_block(b)
        same = seg_col[at, :][:, :1] == seg_ref[...]
        row = lax.broadcasted_iota(jnp.int32, (rows, length), 0) + b * rows
        col = lax.broadcasted_iota(jnp.int32, (rows, length), 1)
        visible = same & (row >= col)
        for h in range(heads):
            cols = slice(h * HD, (h + 1) * HD)
            scores = dot(q_ref[at, cols], k_ref[...], 1, 1) * scale
            masked = jnp.where(visible, scores, -jnp.inf)
            raw = jnp.exp(masked - jnp.max(masked, axis=-1, keepdims=True))
            p_full = raw / jnp.sum(raw, axis=-1, keepdims=True)
            prob[h, at, :] = p_full
            attn[at, cols] = dot(p_full.astype(BF16), v_ref[...], 1, 0).astype(BF16)
        return carry

    lax.fori_loop(0, blocks, forward, 0)
    gsum[...] = jnp.zeros_like(gsum)

    def weight_term(p, which):
        cols = pl.ds(pl.multiple_of(which * depth, depth), depth)
        block = og[behind(p), :, :, cols].reshape(length, depth)
        return dot(block, attn[...], 0, 0).astype(BF16)

    def weight_terms(p):
        xsend[p] = weight_term(p, 1 - core)
        x_copy(p).start()
        part[p] = weight_term(p, core)

    def step(i, carry):
        @pl.when(i + 1 < nchip)
        def _():
            send_own(i + 1)

        done = i - (n - 1)

        @pl.when(done >= 0)
        def _():
            x_copy(done).wait_recv()
            rs_send[done] = (part[done].astype(F32) + xrecv[done].astype(F32)).astype(BF16)
            rs_copy(done).start()

        for s in range(1, n):
            p = i - (s - 1)
            live = (p >= 0) & (p < nchip)

            @pl.when(live & (t >= s))
            def _():
                from_left(p, s).wait_recv()

            @pl.when(live & (t + s < n))
            def _():
                from_right(p, s).wait_recv()

            if s < n - 1:
                @pl.when(live & (t >= s) & has_right)
                def _():
                    go_right(p, s + 1).start()

                @pl.when(live & (t + s < n) & has_left)
                def _():
                    go_left(p, s + 1).start()

        early = i - max(n - 3, 0)

        @pl.when((early >= 0) & (early < nchip - 1))
        def _():
            w_in(early).wait_recv()
            w_across(early).start()

        now = i - (n - 2)

        @pl.when(now >= 0)
        def _():
            w_from_sibling(now).wait_recv()
            j = behind(now)
            gsum[...] += dot(
                og[j].reshape(length, 2 * depth), wfull[j].reshape(2 * depth, width), 1, 0)

            @pl.when(now < nchip - 1)
            def _():
                weight_terms(now)

        return carry

    lax.fori_loop(0, nchip + n - 2, step, 0)

    dk_sum = jnp.zeros((length, HD), F32)
    dv_sum = jnp.zeros((length, HD), F32)

    def backward(b, carry):
        dk_sum, dv_sum = carry
        at = row_block(b)
        for h in range(heads):
            cols = slice(h * HD, (h + 1) * HD)
            gh = gsum[at, cols].astype(BF16)
            p_full = prob[h, at, :]
            delta = jnp.sum(
                gh.astype(F32) * attn[at, cols].astype(F32), axis=-1, keepdims=True)
            dv_sum = dv_sum + dot(p_full.astype(BF16), gh, 0, 0)
            gs = (p_full * (dot(gh, v_ref[...], 1, 1) - delta) * scale).astype(BF16)
            dk_sum = dk_sum + dot(gs, q_ref[at, cols], 0, 0)
            dq_ref[at, cols] = dot(gs, k_ref[...], 1, 0).astype(BF16)
        return dk_sum, dv_sum

    if blocks == 1:
        dk_sum, dv_sum = backward(0, (dk_sum, dv_sum))
    else:
        dk_sum, dv_sum = lax.fori_loop(0, blocks, backward, (dk_sum, dv_sum))
    kv_send[0] = dk_sum.astype(BF16)
    kv_send[1] = dv_sum.astype(BF16)
    kv_copy().start()
    last = nchip - 1
    weight_terms(last)
    kv_copy().wait_recv()
    dk_ref[...] = (dk_sum + kv_recv[0].astype(F32)).astype(BF16)
    dv_ref[...] = (dv_sum + kv_recv[1].astype(F32)).astype(BF16)

    x_copy(last).wait_recv()
    total = part[last].astype(F32) + xrecv[last].astype(F32)
    for p in range(nchip - 1):
        rs_copy(p).wait_recv()
        total = total + rs_recv[p].astype(F32)
    dw_ref[...] = total * (1.0 / (2 * nchip))

    kv_copy().wait_send()

    def drain(p, carry):
        x_copy(p).wait_send()
        w_across(p).wait_send()

        @pl.when(p < nchip - 1)
        def _():
            w_out(p).wait_send()
            rs_copy(p).wait_send()

        for s in range(1, n):
            @pl.when(has_right & (t >= s - 1))
            def _():
                go_right(p, s).wait_send()

            @pl.when(has_left & (t + s - 1 < n))
            def _():
                go_left(p, s).wait_send()

        return carry

    lax.fori_loop(0, nchip, drain, 0)


def local(nchip, n, out_grad, out_weight, queries, keys, values, segment_ids):
    grad, q, k, v = out_grad[0], queries[0], keys[0], values[0]
    rows, model = grad.shape
    depth, width = out_weight.shape
    length = q.shape[0]
    heads = width // HD
    vmem = pl.BlockSpec(memory_space=pltpu.VMEM)
    hbm = pl.BlockSpec(memory_space=pl.ANY)
    dma = pltpu.SemaphoreType.DMA
    most = max(nchip - 1, 1)
    dq, dk, dv, dw = pl.pallas_call(
        functools.partial(kernel, nchip, n),
        out_shape=(
            jax.ShapeDtypeStruct((length, width), BF16),
            jax.ShapeDtypeStruct((length, HD), BF16),
            jax.ShapeDtypeStruct((length, HD), BF16),
            jax.ShapeDtypeStruct((depth, width), F32),
        ),
        in_specs=[hbm, hbm, vmem, vmem, vmem, vmem],
        out_specs=(vmem, vmem, vmem, vmem),
        scratch_shapes=[
            pltpu.VMEM((nchip, n, rows, 2 * depth), BF16),
            pltpu.VMEM((nchip, 2, depth, width), BF16),
            pltpu.VMEM((heads, length, length), F32),
            pltpu.VMEM((length, 128), jnp.int32),
            pltpu.VMEM((length, width), BF16),
            pltpu.VMEM((length, width), F32),
            pltpu.VMEM((2, length, HD), BF16),
            pltpu.VMEM((2, length, HD), BF16),
            pltpu.VMEM((nchip, depth, width), BF16),
            pltpu.VMEM((nchip, depth, width), BF16),
            pltpu.VMEM((nchip, depth, width), BF16),
            pltpu.VMEM((most, depth, width), BF16),
            pltpu.VMEM((most, depth, width), BF16),
            dma((nchip,)), dma,
            dma((nchip, n - 1)), dma((nchip, n - 1)), dma((nchip, n - 1)), dma((nchip, n - 1)),
            dma((most,)), dma((most,)), dma((nchip,)), dma((nchip,)),
            dma((nchip,)), dma((nchip,)), dma((most,)), dma((most,)),
            dma, dma,
        ],
        compiler_params=pltpu.CompilerParams(
            collective_id=0, has_side_effects=True, vmem_limit_bytes=56 << 20),
        cost_estimate=pl.CostEstimate(
            flops=4 * length * model * width, bytes_accessed=8 << 20, transcendentals=0),
    )(grad, out_weight, q, k, v, segment_ids)
    return dq[None], dk[None], dv[None], dw


def solution(mesh):
    in_specs = (
        P("dp", "tensor", None),
        P("dp", "tensor"),
        P("dp", None, "tensor"),
        P("dp", None, "tensor"),
        P("dp", None, "tensor"),
        P("dp", None),
    )
    out_specs = (
        P("dp", None, "tensor"),
        P("dp", None, "tensor"),
        P("dp", None, "tensor"),
        P("dp", "tensor"),
    )
    body = functools.partial(local, mesh.shape["dp"] // 2, mesh.shape["tensor"])
    return jax.shard_map(body, mesh=mesh, in_specs=in_specs, out_specs=out_specs, check_vma=False)
```

```python
import functools

import jax
import jax.numpy as jnp
from jax import lax
from jax.experimental import pallas as pl
from jax.experimental.pallas import tpu as pltpu
from jax.sharding import PartitionSpec as P

HD = 128
MESH = pl.DeviceIdType.MESH
F32 = jnp.float32
BF16 = jnp.bfloat16
ROWS = 256


def dot(a, b, ca, cb):
    return lax.dot_general(a, b, (((ca,), (cb,)), ((), ())), preferred_element_type=F32)


def kernel(
    nchip, n, grad_ref, weight_ref, q_ref, k_ref, v_ref, seg_ref,
    dq_ref, dk_ref, dv_ref, dw_ref,
    og, wfull, prob, seg_col, attn, gsum, kv_send, kv_recv,
    xsend, xrecv, part, rs_send, rs_recv,
    fill_sem, wfill_sem, rsend_sem, rrecv_sem, lsend_sem, lrecv_sem,
    wsend_sem, wrecv_sem, wxsend_sem, wxrecv_sem,
    xsend_sem, xrecv_sem, rss_sem, rsr_sem, kvs_sem, kvr_sem,
):
    d = lax.axis_index("dp")
    t = lax.axis_index("tensor")
    chip, core = d // 2, d % 2
    sibling = (chip * 2 + 1 - core, t)
    partner = (d, t + 1 - 2 * (t % 2))
    length, width = q_ref.shape
    depth = weight_ref.shape[0]
    heads = width // HD
    scale = HD ** (-0.5)
    has_left, has_right = t > 0, t < n - 1

    def behind(p):
        return lax.rem(chip - 1 - p + 2 * nchip, nchip)

    def ahead(p):
        return lax.rem(chip + 1 + p, nchip)

    def fill(j):
        return pltpu.make_async_copy(
            grad_ref.at[:, pl.ds(j * 2 * depth, 2 * depth)], og.at[j, t], fill_sem.at[j]
        )

    def wfill():
        return pltpu.make_async_copy(weight_ref, wfull.at[chip, core], wfill_sem)

    def go_right(p, s):
        at = og.at[behind(p), lax.rem(t - s + 1 + n, n)]
        return pltpu.make_async_remote_copy(
            at, at, rsend_sem.at[p, s - 1], rrecv_sem.at[p, s - 1],
            device_id=(d, lax.rem(t + 1, n)), device_id_type=MESH)

    def from_left(p, s):
        at = og.at[behind(p), lax.rem(t - s + n, n)]
        return pltpu.make_async_remote_copy(
            at, at, rsend_sem.at[p, s - 1], rrecv_sem.at[p, s - 1],
            device_id=(d, lax.rem(t + 1, n)), device_id_type=MESH)

    def go_left(p, s):
        at = og.at[behind(p), lax.rem(t + s - 1, n)]
        return pltpu.make_async_remote_copy(
            at, at, lsend_sem.at[p, s - 1], lrecv_sem.at[p, s - 1],
            device_id=(d, lax.rem(t - 1 + n, n)), device_id_type=MESH)

    def from_right(p, s):
        at = og.at[behind(p), lax.rem(t + s, n)]
        return pltpu.make_async_remote_copy(
            at, at, lsend_sem.at[p, s - 1], lrecv_sem.at[p, s - 1],
            device_id=(d, lax.rem(t - 1 + n, n)), device_id_type=MESH)

    def w_out(p):
        at = wfull.at[chip, core]
        return pltpu.make_async_remote_copy(
            at, at, wsend_sem.at[p], wrecv_sem.at[p],
            device_id=(ahead(p) * 2 + core, t), device_id_type=MESH)

    def w_in(p):
        at = wfull.at[behind(p), core]
        return pltpu.make_async_remote_copy(
            at, at, wsend_sem.at[p], wrecv_sem.at[p],
            device_id=(ahead(p) * 2 + core, t), device_id_type=MESH)

    def w_across(p):
        at = wfull.at[behind(p), core]
        return pltpu.make_async_remote_copy(
            at, at, wxsend_sem.at[p], wxrecv_sem.at[p], device_id=sibling, device_id_type=MESH)

    def w_from_sibling(p):
        at = wfull.at[behind(p), 1 - core]
        return pltpu.make_async_remote_copy(
            at, at, wxsend_sem.at[p], wxrecv_sem.at[p], device_id=sibling, device_id_type=MESH)

    def x_copy(p):
        return pltpu.make_async_remote_copy(
            xsend.at[p], xrecv.at[p], xsend_sem.at[p], xrecv_sem.at[p],
            device_id=sibling, device_id_type=MESH)

    def rs_copy(p):
        return pltpu.make_async_remote_copy(
            rs_send.at[p], rs_recv.at[p], rss_sem.at[p], rsr_sem.at[p],
            device_id=(behind(p) * 2 + core, t), device_id_type=MESH)

    def kv_copy():
        return pltpu.make_async_remote_copy(
            kv_send, kv_recv, kvs_sem, kvr_sem, device_id=partner, device_id_type=MESH)

    def send_own(p):
        @pl.when(has_right)
        def _():
            go_right(p, 1).start()

        @pl.when(has_left)
        def _():
            go_left(p, 1).start()

    for j in range(nchip):
        fill(j).start()
    wfill().start()

    barrier = pltpu.get_barrier_semaphore()

    @pl.when(has_left)
    def _():
        pl.semaphore_signal(barrier, 1, device_id=(d, lax.rem(t - 1 + n, n)), device_id_type=MESH)

    @pl.when(has_right)
    def _():
        pl.semaphore_signal(barrier, 1, device_id=(d, lax.rem(t + 1, n)), device_id_type=MESH)

    pl.semaphore_signal(barrier, 1, device_id=sibling, device_id_type=MESH)
    for p in range(nchip - 1):
        pl.semaphore_signal(barrier, 1, device_id=(ahead(p) * 2 + core, t), device_id_type=MESH)
    inner = has_left & has_right

    @pl.when(inner)
    def _():
        pl.semaphore_wait(barrier, nchip + 2)

    @pl.when(jnp.logical_not(inner))
    def _():
        pl.semaphore_wait(barrier, nchip + 1)

    for j in range(nchip):
        fill(j).wait()
    wfill().wait()
    send_own(0)
    for p in range(nchip - 1):
        w_out(p).start()
    w_across(nchip - 1).start()

    seg_col[...] = jnp.transpose(jnp.broadcast_to(seg_ref[...], (128, length)))
    rows = min(ROWS, length)
    blocks = length // rows

    def row_block(b):
        return pl.ds(pl.multiple_of(b * rows, rows), rows)

    def forward(b, carry):
        at = row_block(b)
        same = seg_col[at, :][:, :1] == seg_ref[...]
        row = lax.broadcasted_iota(jnp.int32, (rows, length), 0) + b * rows
        col = lax.broadcasted_iota(jnp.int32, (rows, length), 1)
        visible = same & (row >= col)
        for h in range(heads):
            cols = slice(h * HD, (h + 1) * HD)
            scores = dot(q_ref[at, cols], k_ref[...], 1, 1) * scale
            masked = jnp.where(visible, scores, -jnp.inf)
            raw = jnp.exp(masked - jnp.max(masked, axis=-1, keepdims=True))
            p_full = raw / jnp.sum(raw, axis=-1, keepdims=True)
            prob[h, at, :] = p_full
            attn[at, cols] = dot(p_full.astype(BF16), v_ref[...], 1, 0).astype(BF16)
        return carry

    lax.fori_loop(0, blocks, forward, 0)
    gsum[...] = jnp.zeros_like(gsum)

    def weight_term(p, which):
        cols = pl.ds(pl.multiple_of(which * depth, depth), depth)
        block = og[behind(p), :, :, cols].reshape(length, depth)
        return dot(block, attn[...], 0, 0).astype(BF16)

    def weight_terms(p):
        xsend[p] = weight_term(p, 1 - core)
        x_copy(p).start()
        part[p] = weight_term(p, core)

    def step(i, carry):
        @pl.when(i + 1 < nchip)
        def _():
            send_own(i + 1)

        done = i - (n - 1)

        @pl.when(done >= 0)
        def _():
            x_copy(done).wait_recv()
            rs_send[done] = (part[done].astype(F32) + xrecv[done].astype(F32)).astype(BF16)
            rs_copy(done).start()

        for s in range(1, n):
            p = i - (s - 1)
            live = (p >= 0) & (p < nchip)

            @pl.when(live & (t >= s))
            def _():
                from_left(p, s).wait_recv()

            @pl.when(live & (t + s < n))
            def _():
                from_right(p, s).wait_recv()

            if s < n - 1:
                @pl.when(live & (t >= s) & has_right)
                def _():
                    go_right(p, s + 1).start()

                @pl.when(live & (t + s < n) & has_left)
                def _():
                    go_left(p, s + 1).start()

        early = i - max(n - 3, 0)

        @pl.when((early >= 0) & (early < nchip - 1))
        def _():
            w_in(early).wait_recv()
            w_across(early).start()

        now = i - (n - 2)

        @pl.when(now >= 0)
        def _():
            w_from_sibling(now).wait_recv()
            j = behind(now)
            gsum[...] += dot(
                og[j].reshape(length, 2 * depth), wfull[j].reshape(2 * depth, width), 1, 0)

            @pl.when(now < nchip - 1)
            def _():
                weight_terms(now)

        return carry

    lax.fori_loop(0, nchip + n - 2, step, 0)

    dk_sum = jnp.zeros((length, HD), F32)
    dv_sum = jnp.zeros((length, HD), F32)

    def backward(b, carry):
        dk_sum, dv_sum = carry
        at = row_block(b)
        for h in range(heads):
            cols = slice(h * HD, (h + 1) * HD)
            gh = gsum[at, cols].astype(BF16)
            p_full = prob[h, at, :]
            delta = jnp.sum(
                gh.astype(F32) * attn[at, cols].astype(F32), axis=-1, keepdims=True)
            dv_sum = dv_sum + dot(p_full.astype(BF16), gh, 0, 0)
            gs = (p_full * (dot(gh, v_ref[...], 1, 1) - delta) * scale).astype(BF16)
            dk_sum = dk_sum + dot(gs, q_ref[at, cols], 0, 0)
            dq_ref[at, cols] = dot(gs, k_ref[...], 1, 0).astype(BF16)
        return dk_sum, dv_sum

    if blocks == 1:
        dk_sum, dv_sum = backward(0, (dk_sum, dv_sum))
    else:
        dk_sum, dv_sum = lax.fori_loop(0, blocks, backward, (dk_sum, dv_sum))
    kv_send[0] = dk_sum.astype(BF16)
    kv_send[1] = dv_sum.astype(BF16)
    kv_copy().start()
    last = nchip - 1
    weight_terms(last)
    kv_copy().wait_recv()
    dk_ref[...] = (dk_sum + kv_recv[0].astype(F32)).astype(BF16)
    dv_ref[...] = (dv_sum + kv_recv[1].astype(F32)).astype(BF16)

    x_copy(last).wait_recv()
    total = part[last].astype(F32) + xrecv[last].astype(F32)
    for p in range(nchip - 1):
        rs_copy(p).wait_recv()
        total = total + rs_recv[p].astype(F32)
    dw_ref[...] = total * (1.0 / (2 * nchip))

    kv_copy().wait_send()

    def drain(p, carry):
        x_copy(p).wait_send()
        w_across(p).wait_send()

        @pl.when(p < nchip - 1)
        def _():
            w_out(p).wait_send()
            rs_copy(p).wait_send()

        for s in range(1, n):
            @pl.when(has_right & (t >= s - 1))
            def _():
                go_right(p, s).wait_send()

            @pl.when(has_left & (t + s - 1 < n))
            def _():
                go_left(p, s).wait_send()

        return carry

    lax.fori_loop(0, nchip, drain, 0)


def hand_out(*refs):
    sources, results, sems = refs[:4], refs[4:8], refs[8]
    copies = [
        pltpu.make_async_copy(a, b, sems.at[i]) for i, (a, b) in enumerate(zip(sources, results))
    ]
    for copy in copies:
        copy.start()
    for copy in copies:
        copy.wait()


def local(nchip, n, out_grad, out_weight, queries, keys, values, segment_ids):
    grad, q, k, v = out_grad[0], queries[0], keys[0], values[0]
    rows, model = grad.shape
    depth, width = out_weight.shape
    length = q.shape[0]
    heads = width // HD
    vmem = pl.BlockSpec(memory_space=pltpu.VMEM)
    hbm = pl.BlockSpec(memory_space=pl.ANY)
    dma = pltpu.SemaphoreType.DMA
    most = max(nchip - 1, 1)
    results = pl.pallas_call(
        functools.partial(kernel, nchip, n),
        out_shape=(
            jax.ShapeDtypeStruct((length, width), BF16),
            jax.ShapeDtypeStruct((length, HD), BF16),
            jax.ShapeDtypeStruct((length, HD), BF16),
            jax.ShapeDtypeStruct((depth, width), F32),
        ),
        in_specs=[hbm, hbm, vmem, vmem, vmem, vmem],
        out_specs=(vmem, vmem, vmem, vmem),
        scratch_shapes=[
            pltpu.VMEM((nchip, n, rows, 2 * depth), BF16),
            pltpu.VMEM((nchip, 2, depth, width), BF16),
            pltpu.VMEM((heads, length, length), F32),
            pltpu.VMEM((length, 128), jnp.int32),
            pltpu.VMEM((length, width), BF16),
            pltpu.VMEM((length, width), F32),
            pltpu.VMEM((2, length, HD), BF16),
            pltpu.VMEM((2, length, HD), BF16),
            pltpu.VMEM((nchip, depth, width), BF16),
            pltpu.VMEM((nchip, depth, width), BF16),
            pltpu.VMEM((nchip, depth, width), BF16),
            pltpu.VMEM((most, depth, width), BF16),
            pltpu.VMEM((most, depth, width), BF16),
            dma((nchip,)), dma,
            dma((nchip, n - 1)), dma((nchip, n - 1)), dma((nchip, n - 1)), dma((nchip, n - 1)),
            dma((most,)), dma((most,)), dma((nchip,)), dma((nchip,)),
            dma((nchip,)), dma((nchip,)), dma((most,)), dma((most,)),
            dma, dma,
        ],
        compiler_params=pltpu.CompilerParams(
            collective_id=0, has_side_effects=True, vmem_limit_bytes=56 << 20),
        cost_estimate=pl.CostEstimate(
            flops=4 * length * model * width, bytes_accessed=8 << 20, transcendentals=0),
    )(grad, out_weight, q, k, v, segment_ids)
    dq, dk, dv, dw = pl.pallas_call(
        hand_out,
        out_shape=tuple(jax.ShapeDtypeStruct(r.shape, r.dtype) for r in results),
        in_specs=[hbm] * 4,
        out_specs=(hbm,) * 4,
        scratch_shapes=[dma((4,))],
    )(*results)
    return dq[None], dk[None], dv[None], dw


def solution(mesh):
    in_specs = (
        P("dp", "tensor", None),
        P("dp", "tensor"),
        P("dp", None, "tensor"),
        P("dp", None, "tensor"),
        P("dp", None, "tensor"),
        P("dp", None),
    )
    out_specs = (
        P("dp", None, "tensor"),
        P("dp", None, "tensor"),
        P("dp", None, "tensor"),
        P("dp", "tensor"),
    )
    body = functools.partial(local, mesh.shape["dp"] // 2, mesh.shape["tensor"])
    return jax.shard_map(body, mesh=mesh, in_specs=in_specs, out_specs=out_specs, check_vma=False)
```

```python
import functools

import jax
import jax.numpy as jnp
from jax import lax
from jax.experimental import pallas as pl
from jax.experimental.pallas import tpu as pltpu
from jax.sharding import PartitionSpec as P

HD = 128
MESH = pl.DeviceIdType.MESH
F32 = jnp.float32
BF16 = jnp.bfloat16
ROWS = 256


def dot(a, b, ca, cb):
    return lax.dot_general(a, b, (((ca,), (cb,)), ((), ())), preferred_element_type=F32)


def kernel(
    nchip, n, grad_ref, weight_ref, q_ref, k_ref, v_ref, seg_ref,
    dq_ref, dk_ref, dv_ref, dw_ref,
    og, wfull, prob, seg_col, attn, gsum, kv_send, kv_recv,
    xsend, xrecv, part, rs_send, rs_recv,
    fill_sem, wfill_sem, rsend_sem, rrecv_sem, lsend_sem, lrecv_sem,
    wsend_sem, wrecv_sem, wxsend_sem, wxrecv_sem,
    xsend_sem, xrecv_sem, rss_sem, rsr_sem, kvs_sem, kvr_sem,
):
    d = lax.axis_index("dp")
    t = lax.axis_index("tensor")
    chip, core = d // 2, d % 2
    sibling = (chip * 2 + 1 - core, t)
    partner = (d, t + 1 - 2 * (t % 2))
    length, width = q_ref.shape
    depth = weight_ref.shape[0]
    heads = width // HD
    scale = HD ** (-0.5)
    has_left, has_right = t > 0, t < n - 1

    def behind(p):
        return lax.rem(chip - 1 - p + 2 * nchip, nchip)

    def ahead(p):
        return lax.rem(chip + 1 + p, nchip)

    def fill(j):
        return pltpu.make_async_copy(
            grad_ref.at[:, pl.ds(j * 2 * depth, 2 * depth)], og.at[j, t], fill_sem.at[j]
        )

    def wfill():
        return pltpu.make_async_copy(weight_ref, wfull.at[chip, core], wfill_sem)

    def go_right(p, s):
        at = og.at[behind(p), lax.rem(t - s + 1 + n, n)]
        return pltpu.make_async_remote_copy(
            at, at, rsend_sem.at[p, s - 1], rrecv_sem.at[p, s - 1],
            device_id=(d, lax.rem(t + 1, n)), device_id_type=MESH)

    def from_left(p, s):
        at = og.at[behind(p), lax.rem(t - s + n, n)]
        return pltpu.make_async_remote_copy(
            at, at, rsend_sem.at[p, s - 1], rrecv_sem.at[p, s - 1],
            device_id=(d, lax.rem(t + 1, n)), device_id_type=MESH)

    def go_left(p, s):
        at = og.at[behind(p), lax.rem(t + s - 1, n)]
        return pltpu.make_async_remote_copy(
            at, at, lsend_sem.at[p, s - 1], lrecv_sem.at[p, s - 1],
            device_id=(d, lax.rem(t - 1 + n, n)), device_id_type=MESH)

    def from_right(p, s):
        at = og.at[behind(p), lax.rem(t + s, n)]
        return pltpu.make_async_remote_copy(
            at, at, lsend_sem.at[p, s - 1], lrecv_sem.at[p, s - 1],
            device_id=(d, lax.rem(t - 1 + n, n)), device_id_type=MESH)

    def w_out(p):
        at = wfull.at[chip, core]
        return pltpu.make_async_remote_copy(
            at, at, wsend_sem.at[p], wrecv_sem.at[p],
            device_id=(ahead(p) * 2 + core, t), device_id_type=MESH)

    def w_in(p):
        at = wfull.at[behind(p), core]
        return pltpu.make_async_remote_copy(
            at, at, wsend_sem.at[p], wrecv_sem.at[p],
            device_id=(ahead(p) * 2 + core, t), device_id_type=MESH)

    def w_across(p):
        at = wfull.at[behind(p), core]
        return pltpu.make_async_remote_copy(
            at, at, wxsend_sem.at[p], wxrecv_sem.at[p], device_id=sibling, device_id_type=MESH)

    def w_from_sibling(p):
        at = wfull.at[behind(p), 1 - core]
        return pltpu.make_async_remote_copy(
            at, at, wxsend_sem.at[p], wxrecv_sem.at[p], device_id=sibling, device_id_type=MESH)

    def x_copy(p):
        return pltpu.make_async_remote_copy(
            xsend.at[p], xrecv.at[p], xsend_sem.at[p], xrecv_sem.at[p],
            device_id=sibling, device_id_type=MESH)

    def rs_copy(p):
        return pltpu.make_async_remote_copy(
            rs_send.at[p], rs_recv.at[p], rss_sem.at[p], rsr_sem.at[p],
            device_id=(behind(p) * 2 + core, t), device_id_type=MESH)

    def kv_copy():
        return pltpu.make_async_remote_copy(
            kv_send, kv_recv, kvs_sem, kvr_sem, device_id=partner, device_id_type=MESH)

    def send_own(p):
        @pl.when(has_right)
        def _():
            go_right(p, 1).start()

        @pl.when(has_left)
        def _():
            go_left(p, 1).start()

    for j in range(nchip):
        fill(j).start()
    wfill().start()

    barrier = pltpu.get_barrier_semaphore()

    @pl.when(has_left)
    def _():
        pl.semaphore_signal(barrier, 1, device_id=(d, lax.rem(t - 1 + n, n)), device_id_type=MESH)

    @pl.when(has_right)
    def _():
        pl.semaphore_signal(barrier, 1, device_id=(d, lax.rem(t + 1, n)), device_id_type=MESH)

    pl.semaphore_signal(barrier, 1, device_id=sibling, device_id_type=MESH)
    for p in range(nchip - 1):
        pl.semaphore_signal(barrier, 1, device_id=(ahead(p) * 2 + core, t), device_id_type=MESH)
    inner = has_left & has_right

    @pl.when(inner)
    def _():
        pl.semaphore_wait(barrier, nchip + 2)

    @pl.when(jnp.logical_not(inner))
    def _():
        pl.semaphore_wait(barrier, nchip + 1)

    for j in range(nchip):
        fill(j).wait()
    wfill().wait()
    send_own(0)
    for p in range(nchip - 1):
        w_out(p).start()
    w_across(nchip - 1).start()

    seg_col[...] = jnp.transpose(jnp.broadcast_to(seg_ref[...], (128, length)))
    rows = min(ROWS, length)
    blocks = length // rows

    def row_block(b):
        return pl.ds(pl.multiple_of(b * rows, rows), rows)

    def forward(b, carry):
        at = row_block(b)
        same = seg_col[at, :][:, :1] == seg_ref[...]
        row = lax.broadcasted_iota(jnp.int32, (rows, length), 0) + b * rows
        col = lax.broadcasted_iota(jnp.int32, (rows, length), 1)
        visible = same & (row >= col)
        for h in range(heads):
            cols = slice(h * HD, (h + 1) * HD)
            scores = dot(q_ref[at, cols], k_ref[...], 1, 1) * scale
            masked = jnp.where(visible, scores, -jnp.inf)
            raw = jnp.exp(masked - jnp.max(masked, axis=-1, keepdims=True))
            p_full = raw / jnp.sum(raw, axis=-1, keepdims=True)
            prob[h, at, :] = p_full
            attn[at, cols] = dot(p_full.astype(BF16), v_ref[...], 1, 0).astype(BF16)
        return carry

    lax.fori_loop(0, blocks, forward, 0)
    gsum[...] = jnp.zeros_like(gsum)

    def weight_term(p, which):
        cols = pl.ds(pl.multiple_of(which * depth, depth), depth)
        block = og[behind(p), :, :, cols].reshape(length, depth)
        return dot(block, attn[...], 0, 0).astype(BF16)

    def weight_terms(p):
        xsend[p] = weight_term(p, 1 - core)
        x_copy(p).start()
        part[p] = weight_term(p, core)

    def step(i, carry):
        @pl.when(i + 1 < nchip)
        def _():
            send_own(i + 1)

        done = i - (n - 1)

        @pl.when(done >= 0)
        def _():
            x_copy(done).wait_recv()
            rs_send[done] = (part[done].astype(F32) + xrecv[done].astype(F32)).astype(BF16)
            rs_copy(done).start()

        for s in range(1, n):
            p = i - (s - 1)
            live = (p >= 0) & (p < nchip)

            @pl.when(live & (t >= s))
            def _():
                from_left(p, s).wait_recv()

            @pl.when(live & (t + s < n))
            def _():
                from_right(p, s).wait_recv()

            if s < n - 1:
                @pl.when(live & (t >= s) & has_right)
                def _():
                    go_right(p, s + 1).start()

                @pl.when(live & (t + s < n) & has_left)
                def _():
                    go_left(p, s + 1).start()

        early = i - max(n - 3, 0)

        @pl.when((early >= 0) & (early < nchip - 1))
        def _():
            w_in(early).wait_recv()
            w_across(early).start()

        now = i - (n - 2)

        @pl.when(now >= 0)
        def _():
            w_from_sibling(now).wait_recv()
            j = behind(now)
            gsum[...] += dot(
                og[j].reshape(length, 2 * depth), wfull[j].reshape(2 * depth, width), 1, 0)

            @pl.when(now < nchip - 1)
            def _():
                weight_terms(now)

        return carry

    lax.fori_loop(0, nchip + n - 2, step, 0)

    dk_sum = jnp.zeros((length, HD), F32)
    dv_sum = jnp.zeros((length, HD), F32)

    def backward(b, carry):
        dk_sum, dv_sum = carry
        at = row_block(b)
        for h in range(heads):
            cols = slice(h * HD, (h + 1) * HD)
            gh = gsum[at, cols].astype(BF16)
            p_full = prob[h, at, :]
            delta = jnp.sum(
                gh.astype(F32) * attn[at, cols].astype(F32), axis=-1, keepdims=True)
            dv_sum = dv_sum + dot(p_full.astype(BF16), gh, 0, 0)
            gs = (p_full * (dot(gh, v_ref[...], 1, 1) - delta) * scale).astype(BF16)
            dk_sum = dk_sum + dot(gs, q_ref[at, cols], 0, 0)
            dq_ref[at, cols] = dot(gs, k_ref[...], 1, 0).astype(BF16)
        return dk_sum, dv_sum

    if blocks == 1:
        dk_sum, dv_sum = backward(0, (dk_sum, dv_sum))
    else:
        dk_sum, dv_sum = lax.fori_loop(0, blocks, backward, (dk_sum, dv_sum))
    kv_send[0] = dk_sum.astype(BF16)
    kv_send[1] = dv_sum.astype(BF16)
    kv_copy().start()
    last = nchip - 1
    weight_terms(last)
    kv_copy().wait_recv()
    dk_ref[...] = (dk_sum + kv_recv[0].astype(F32)).astype(BF16)
    dv_ref[...] = (dv_sum + kv_recv[1].astype(F32)).astype(BF16)

    x_copy(last).wait_recv()
    total = part[last].astype(F32) + xrecv[last].astype(F32)
    for p in range(nchip - 1):
        rs_copy(p).wait_recv()
        total = total + rs_recv[p].astype(F32)
    dw_ref[...] = total * (1.0 / (2 * nchip))

    kv_copy().wait_send()

    def drain(p, carry):
        x_copy(p).wait_send()
        w_across(p).wait_send()

        @pl.when(p < nchip - 1)
        def _():
            w_out(p).wait_send()
            rs_copy(p).wait_send()

        for s in range(1, n):
            @pl.when(has_right & (t >= s - 1))
            def _():
                go_right(p, s).wait_send()

            @pl.when(has_left & (t + s - 1 < n))
            def _():
                go_left(p, s).wait_send()

        return carry

    lax.fori_loop(0, nchip, drain, 0)


def hand_out(*refs):
    for source, result in zip(refs[:4], refs[4:]):
        result[...] = source[...]


def local(nchip, n, out_grad, out_weight, queries, keys, values, segment_ids):
    grad, q, k, v = out_grad[0], queries[0], keys[0], values[0]
    rows, model = grad.shape
    depth, width = out_weight.shape
    length = q.shape[0]
    heads = width // HD
    vmem = pl.BlockSpec(memory_space=pltpu.VMEM)
    hbm = pl.BlockSpec(memory_space=pl.ANY)
    dma = pltpu.SemaphoreType.DMA
    most = max(nchip - 1, 1)
    results = pl.pallas_call(
        functools.partial(kernel, nchip, n),
        out_shape=(
            jax.ShapeDtypeStruct((length, width), BF16),
            jax.ShapeDtypeStruct((length, HD), BF16),
            jax.ShapeDtypeStruct((length, HD), BF16),
            jax.ShapeDtypeStruct((depth, width), F32),
        ),
        in_specs=[hbm, hbm, vmem, vmem, vmem, vmem],
        out_specs=(vmem, vmem, vmem, vmem),
        scratch_shapes=[
            pltpu.VMEM((nchip, n, rows, 2 * depth), BF16),
            pltpu.VMEM((nchip, 2, depth, width), BF16),
            pltpu.VMEM((heads, length, length), F32),
            pltpu.VMEM((length, 128), jnp.int32),
            pltpu.VMEM((length, width), BF16),
            pltpu.VMEM((length, width), F32),
            pltpu.VMEM((2, length, HD), BF16),
            pltpu.VMEM((2, length, HD), BF16),
            pltpu.VMEM((nchip, depth, width), BF16),
            pltpu.VMEM((nchip, depth, width), BF16),
            pltpu.VMEM((nchip, depth, width), BF16),
            pltpu.VMEM((most, depth, width), BF16),
            pltpu.VMEM((most, depth, width), BF16),
            dma((nchip,)), dma,
            dma((nchip, n - 1)), dma((nchip, n - 1)), dma((nchip, n - 1)), dma((nchip, n - 1)),
            dma((most,)), dma((most,)), dma((nchip,)), dma((nchip,)),
            dma((nchip,)), dma((nchip,)), dma((most,)), dma((most,)),
            dma, dma,
        ],
        compiler_params=pltpu.CompilerParams(
            collective_id=0, has_side_effects=True, vmem_limit_bytes=56 << 20),
        cost_estimate=pl.CostEstimate(
            flops=4 * length * model * width, bytes_accessed=8 << 20, transcendentals=0),
    )(grad, out_weight, q, k, v, segment_ids)
    dq, dk, dv, dw = pl.pallas_call(
        hand_out,
        out_shape=tuple(jax.ShapeDtypeStruct(r.shape, r.dtype) for r in results),
        in_specs=[vmem] * 4,
        out_specs=(vmem,) * 4,
    )(*results)
    return dq[None], dk[None], dv[None], dw


def solution(mesh):
    in_specs = (
        P("dp", "tensor", None),
        P("dp", "tensor"),
        P("dp", None, "tensor"),
        P("dp", None, "tensor"),
        P("dp", None, "tensor"),
        P("dp", None),
    )
    out_specs = (
        P("dp", None, "tensor"),
        P("dp", None, "tensor"),
        P("dp", None, "tensor"),
        P("dp", "tensor"),
    )
    body = functools.partial(local, mesh.shape["dp"] // 2, mesh.shape["tensor"])
    return jax.shard_map(body, mesh=mesh, in_specs=in_specs, out_specs=out_specs, check_vma=False)
```

```python
import functools

import jax
import jax.numpy as jnp
from jax import lax
from jax.experimental import pallas as pl
from jax.experimental.pallas import tpu as pltpu
from jax.sharding import PartitionSpec as P

HD = 128
MESH = pl.DeviceIdType.MESH
F32 = jnp.float32
BF16 = jnp.bfloat16
ROWS = 256


def dot(a, b, ca, cb):
    return lax.dot_general(a, b, (((ca,), (cb,)), ((), ())), preferred_element_type=F32)


def kernel(
    nchip, n, grad_ref, weight_ref, q_ref, k_ref, v_ref, seg_ref,
    dq_ref, dk_ref, dv_ref, dw_ref,
    og, wfull, prob, seg_col, attn, gsum, kv_send, kv_recv,
    xsend, xrecv, part, rs_send, rs_recv,
    fill_sem, wfill_sem, rsend_sem, rrecv_sem, lsend_sem, lrecv_sem,
    wsend_sem, wrecv_sem, wxsend_sem, wxrecv_sem,
    xsend_sem, xrecv_sem, rss_sem, rsr_sem, kvs_sem, kvr_sem,
):
    d = lax.axis_index("dp")
    t = lax.axis_index("tensor")
    chip, core = d // 2, d % 2
    sibling = (chip * 2 + 1 - core, t)
    partner = (d, t + 1 - 2 * (t % 2))
    length, width = q_ref.shape
    depth = weight_ref.shape[0]
    heads = width // HD
    scale = HD ** (-0.5)
    has_left, has_right = t > 0, t < n - 1

    def behind(p):
        return lax.rem(chip - 1 - p + 2 * nchip, nchip)

    def ahead(p):
        return lax.rem(chip + 1 + p, nchip)

    def fill(c):
        return pltpu.make_async_copy(
            grad_ref.at[:, pl.ds(c * depth, depth)], og.at[c // 2, c % 2, t], fill_sem.at[c]
        )

    def wfill():
        return pltpu.make_async_copy(weight_ref, wfull.at[chip, core], wfill_sem)

    def go_right(p, s):
        at = og.at[behind(p // 2), p % 2, lax.rem(t - s + 1 + n, n)]
        return pltpu.make_async_remote_copy(
            at, at, rsend_sem.at[p, s - 1], rrecv_sem.at[p, s - 1],
            device_id=(d, lax.rem(t + 1, n)), device_id_type=MESH)

    def from_left(p, s):
        at = og.at[behind(p // 2), p % 2, lax.rem(t - s + n, n)]
        return pltpu.make_async_remote_copy(
            at, at, rsend_sem.at[p, s - 1], rrecv_sem.at[p, s - 1],
            device_id=(d, lax.rem(t + 1, n)), device_id_type=MESH)

    def go_left(p, s):
        at = og.at[behind(p // 2), p % 2, lax.rem(t + s - 1, n)]
        return pltpu.make_async_remote_copy(
            at, at, lsend_sem.at[p, s - 1], lrecv_sem.at[p, s - 1],
            device_id=(d, lax.rem(t - 1 + n, n)), device_id_type=MESH)

    def from_right(p, s):
        at = og.at[behind(p // 2), p % 2, lax.rem(t + s, n)]
        return pltpu.make_async_remote_copy(
            at, at, lsend_sem.at[p, s - 1], lrecv_sem.at[p, s - 1],
            device_id=(d, lax.rem(t - 1 + n, n)), device_id_type=MESH)

    def w_out(p):
        at = wfull.at[chip, core]
        return pltpu.make_async_remote_copy(
            at, at, wsend_sem.at[p], wrecv_sem.at[p],
            device_id=(ahead(p) * 2 + core, t), device_id_type=MESH)

    def w_in(p):
        at = wfull.at[behind(p), core]
        return pltpu.make_async_remote_copy(
            at, at, wsend_sem.at[p], wrecv_sem.at[p],
            device_id=(ahead(p) * 2 + core, t), device_id_type=MESH)

    def w_across(p):
        at = wfull.at[behind(p), core]
        return pltpu.make_async_remote_copy(
            at, at, wxsend_sem.at[p], wxrecv_sem.at[p], device_id=sibling, device_id_type=MESH)

    def w_from_sibling(p):
        at = wfull.at[behind(p), 1 - core]
        return pltpu.make_async_remote_copy(
            at, at, wxsend_sem.at[p], wxrecv_sem.at[p], device_id=sibling, device_id_type=MESH)

    def x_copy(p):
        return pltpu.make_async_remote_copy(
            xsend.at[p], xrecv.at[p], xsend_sem.at[p], xrecv_sem.at[p],
            device_id=sibling, device_id_type=MESH)

    def rs_copy(p):
        return pltpu.make_async_remote_copy(
            rs_send.at[p], rs_recv.at[p], rss_sem.at[p], rsr_sem.at[p],
            device_id=(behind(p) * 2 + core, t), device_id_type=MESH)

    def kv_copy():
        return pltpu.make_async_remote_copy(
            kv_send, kv_recv, kvs_sem, kvr_sem, device_id=partner, device_id_type=MESH)

    def send_own(p):
        @pl.when(has_right)
        def _():
            go_right(p, 1).start()

        @pl.when(has_left)
        def _():
            go_left(p, 1).start()

    for j in range(2 * nchip):
        fill(j).start()
    wfill().start()

    barrier = pltpu.get_barrier_semaphore()

    @pl.when(has_left)
    def _():
        pl.semaphore_signal(barrier, 1, device_id=(d, lax.rem(t - 1 + n, n)), device_id_type=MESH)

    @pl.when(has_right)
    def _():
        pl.semaphore_signal(barrier, 1, device_id=(d, lax.rem(t + 1, n)), device_id_type=MESH)

    pl.semaphore_signal(barrier, 1, device_id=sibling, device_id_type=MESH)
    for p in range(nchip - 1):
        pl.semaphore_signal(barrier, 1, device_id=(ahead(p) * 2 + core, t), device_id_type=MESH)
    inner = has_left & has_right

    @pl.when(inner)
    def _():
        pl.semaphore_wait(barrier, nchip + 2)

    @pl.when(jnp.logical_not(inner))
    def _():
        pl.semaphore_wait(barrier, nchip + 1)

    for j in range(2 * nchip):
        fill(j).wait()
    wfill().wait()
    for p in range(min(4, 2 * nchip)):
        send_own(p)
    for p in range(nchip - 1):
        w_out(p).start()
    w_across(nchip - 1).start()

    seg_col[...] = jnp.transpose(jnp.broadcast_to(seg_ref[...], (128, length)))
    rows = min(ROWS, length)
    blocks = length // rows

    def row_block(b):
        return pl.ds(pl.multiple_of(b * rows, rows), rows)

    def forward(b, carry):
        at = row_block(b)
        same = seg_col[at, :][:, :1] == seg_ref[...]
        row = lax.broadcasted_iota(jnp.int32, (rows, length), 0) + b * rows
        col = lax.broadcasted_iota(jnp.int32, (rows, length), 1)
        visible = same & (row >= col)
        for h in range(heads):
            cols = slice(h * HD, (h + 1) * HD)
            scores = dot(q_ref[at, cols], k_ref[...], 1, 1) * scale
            masked = jnp.where(visible, scores, -jnp.inf)
            raw = jnp.exp(masked - jnp.max(masked, axis=-1, keepdims=True))
            p_full = raw / jnp.sum(raw, axis=-1, keepdims=True)
            prob[h, at, :] = p_full
            attn[at, cols] = dot(p_full.astype(BF16), v_ref[...], 1, 0).astype(BF16)
        return carry

    lax.fori_loop(0, blocks, forward, 0)
    gsum[...] = jnp.zeros_like(gsum)

    def weight_term(p, which):
        block = og[behind(p), which].reshape(length, depth)
        return dot(block, attn[...], 0, 0).astype(BF16)

    def weight_terms(p):
        xsend[p] = weight_term(p, 1 - core)
        x_copy(p).start()
        part[p] = weight_term(p, core)

    def step(i, carry):
        @pl.when(i + 4 < 2 * nchip)
        def _():
            send_own(i + 4)

        done = i - n

        @pl.when((done >= 0) & (done % 2 == 0))
        def _():
            p = done // 2
            x_copy(p).wait_recv()
            rs_send[p] = (part[p].astype(F32) + xrecv[p].astype(F32)).astype(BF16)
            rs_copy(p).start()

        for s in range(1, n):
            p = i - (s - 1)
            live = (p >= 0) & (p < 2 * nchip)

            @pl.when(live & (t >= s))
            def _():
                from_left(p, s).wait_recv()

            @pl.when(live & (t + s < n))
            def _():
                from_right(p, s).wait_recv()

            if s < n - 1:
                @pl.when(live & (t >= s) & has_right)
                def _():
                    go_right(p, s + 1).start()

                @pl.when(live & (t + s < n) & has_left)
                def _():
                    go_left(p, s + 1).start()

        early = i - max(n - 3, 0)

        @pl.when((early >= 0) & (early < 2 * (nchip - 1)) & (early % 2 == 0))
        def _():
            w_in(early // 2).wait_recv()
            w_across(early // 2).start()

        now = i - (n - 2)

        @pl.when(now >= 0)
        def _():
            p, half = now // 2, now % 2

            @pl.when(half == 0)
            def _():
                w_from_sibling(p).wait_recv()

            j = behind(p)
            gsum[...] += dot(og[j, half].reshape(length, depth), wfull[j, half], 1, 0)

            @pl.when((half == 1) & (p < nchip - 1))
            def _():
                weight_terms(p)

        return carry

    lax.fori_loop(0, 2 * nchip + n - 2, step, 0)

    dk_sum = jnp.zeros((length, HD), F32)
    dv_sum = jnp.zeros((length, HD), F32)

    def backward(b, carry):
        dk_sum, dv_sum = carry
        at = row_block(b)
        for h in range(heads):
            cols = slice(h * HD, (h + 1) * HD)
            gh = gsum[at, cols].astype(BF16)
            p_full = prob[h, at, :]
            delta = jnp.sum(
                gh.astype(F32) * attn[at, cols].astype(F32), axis=-1, keepdims=True)
            dv_sum = dv_sum + dot(p_full.astype(BF16), gh, 0, 0)
            gs = (p_full * (dot(gh, v_ref[...], 1, 1) - delta) * scale).astype(BF16)
            dk_sum = dk_sum + dot(gs, q_ref[at, cols], 0, 0)
            dq_ref[at, cols] = dot(gs, k_ref[...], 1, 0).astype(BF16)
        return dk_sum, dv_sum

    if blocks == 1:
        dk_sum, dv_sum = backward(0, (dk_sum, dv_sum))
    else:
        dk_sum, dv_sum = lax.fori_loop(0, blocks, backward, (dk_sum, dv_sum))
    kv_send[0] = dk_sum.astype(BF16)
    kv_send[1] = dv_sum.astype(BF16)
    kv_copy().start()
    last = nchip - 1
    weight_terms(last)
    kv_copy().wait_recv()
    dk_ref[...] = (dk_sum + kv_recv[0].astype(F32)).astype(BF16)
    dv_ref[...] = (dv_sum + kv_recv[1].astype(F32)).astype(BF16)

    x_copy(last).wait_recv()
    total = part[last].astype(F32) + xrecv[last].astype(F32)
    for p in range(nchip - 1):
        rs_copy(p).wait_recv()
        total = total + rs_recv[p].astype(F32)
    dw_ref[...] = total * (1.0 / (2 * nchip))

    kv_copy().wait_send()

    def drain(p, carry):
        x_copy(p).wait_send()
        w_across(p).wait_send()

        @pl.when(p < nchip - 1)
        def _():
            w_out(p).wait_send()
            rs_copy(p).wait_send()

        return carry

    def drain_line(p, carry):
        for s in range(1, n):
            @pl.when(has_right & (t >= s - 1))
            def _():
                go_right(p, s).wait_send()

            @pl.when(has_left & (t + s - 1 < n))
            def _():
                go_left(p, s).wait_send()

        return carry

    lax.fori_loop(0, 2 * nchip, drain_line, 0)
    lax.fori_loop(0, nchip, drain, 0)


def hand_out(*refs):
    for source, result in zip(refs[:4], refs[4:]):
        result[...] = source[...]


def local(nchip, n, out_grad, out_weight, queries, keys, values, segment_ids):
    grad, q, k, v = out_grad[0], queries[0], keys[0], values[0]
    rows, model = grad.shape
    depth, width = out_weight.shape
    length = q.shape[0]
    heads = width // HD
    vmem = pl.BlockSpec(memory_space=pltpu.VMEM)
    hbm = pl.BlockSpec(memory_space=pl.ANY)
    dma = pltpu.SemaphoreType.DMA
    most = max(nchip - 1, 1)
    results = pl.pallas_call(
        functools.partial(kernel, nchip, n),
        out_shape=(
            jax.ShapeDtypeStruct((length, width), BF16),
            jax.ShapeDtypeStruct((length, HD), BF16),
            jax.ShapeDtypeStruct((length, HD), BF16),
            jax.ShapeDtypeStruct((depth, width), F32),
        ),
        in_specs=[hbm, hbm, vmem, vmem, vmem, vmem],
        out_specs=(vmem, vmem, vmem, vmem),
        scratch_shapes=[
            pltpu.VMEM((nchip, 2, n, rows, depth), BF16),
            pltpu.VMEM((nchip, 2, depth, width), BF16),
            pltpu.VMEM((heads, length, length), F32),
            pltpu.VMEM((length, 128), jnp.int32),
            pltpu.VMEM((length, width), BF16),
            pltpu.VMEM((length, width), F32),
            pltpu.VMEM((2, length, HD), BF16),
            pltpu.VMEM((2, length, HD), BF16),
            pltpu.VMEM((nchip, depth, width), BF16),
            pltpu.VMEM((nchip, depth, width), BF16),
            pltpu.VMEM((nchip, depth, width), BF16),
            pltpu.VMEM((most, depth, width), BF16),
            pltpu.VMEM((most, depth, width), BF16),
            dma((2 * nchip,)), dma,
            dma((2 * nchip, n - 1)), dma((2 * nchip, n - 1)),
            dma((2 * nchip, n - 1)), dma((2 * nchip, n - 1)),
            dma((most,)), dma((most,)), dma((nchip,)), dma((nchip,)),
            dma((nchip,)), dma((nchip,)), dma((most,)), dma((most,)),
            dma, dma,
        ],
        compiler_params=pltpu.CompilerParams(
            collective_id=0, has_side_effects=True, vmem_limit_bytes=56 << 20),
        cost_estimate=pl.CostEstimate(
            flops=4 * length * model * width, bytes_accessed=8 << 20, transcendentals=0),
    )(grad, out_weight, q, k, v, segment_ids)
    dq, dk, dv, dw = pl.pallas_call(
        hand_out,
        out_shape=tuple(jax.ShapeDtypeStruct(r.shape, r.dtype) for r in results),
        in_specs=[vmem] * 4,
        out_specs=(vmem,) * 4,
    )(*results)
    return dq[None], dk[None], dv[None], dw


def solution(mesh):
    in_specs = (
        P("dp", "tensor", None),
        P("dp", "tensor"),
        P("dp", None, "tensor"),
        P("dp", None, "tensor"),
        P("dp", None, "tensor"),
        P("dp", None),
    )
    out_specs = (
        P("dp", None, "tensor"),
        P("dp", None, "tensor"),
        P("dp", None, "tensor"),
        P("dp", "tensor"),
    )
    body = functools.partial(local, mesh.shape["dp"] // 2, mesh.shape["tensor"])
    return jax.shard_map(body, mesh=mesh, in_specs=in_specs, out_specs=out_specs, check_vma=False)
```

```python
import functools

import jax
import jax.numpy as jnp
from jax import lax
from jax.experimental import pallas as pl
from jax.experimental.pallas import tpu as pltpu
from jax.sharding import PartitionSpec as P

HD = 128
MESH = pl.DeviceIdType.MESH
F32 = jnp.float32
BF16 = jnp.bfloat16
ROWS = 256


def dot(a, b, ca, cb):
    return lax.dot_general(a, b, (((ca,), (cb,)), ((), ())), preferred_element_type=F32)


def kernel(
    nchip, n, grad_ref, weight_ref, q_ref, k_ref, v_ref, seg_ref,
    dq_ref, dk_ref, dv_ref, dw_ref,
    og, wfull, prob, score_grad, seg_col, attn, gsum, kv_send, kv_recv,
    xsend, xrecv, part, rs_send, rs_recv,
    fill_sem, wfill_sem, rsend_sem, rrecv_sem, lsend_sem, lrecv_sem,
    wsend_sem, wrecv_sem, wxsend_sem, wxrecv_sem,
    xsend_sem, xrecv_sem, rss_sem, rsr_sem, kvs_sem, kvr_sem,
):
    d = lax.axis_index("dp")
    t = lax.axis_index("tensor")
    chip, core = d // 2, d % 2
    sibling = (chip * 2 + 1 - core, t)
    partner = (d, t + 1 - 2 * (t % 2))
    length, width = q_ref.shape
    depth = weight_ref.shape[0]
    heads = width // HD
    scale = HD ** (-0.5)
    has_left, has_right = t > 0, t < n - 1

    def behind(p):
        return lax.rem(chip - 1 - p + 2 * nchip, nchip)

    def ahead(p):
        return lax.rem(chip + 1 + p, nchip)

    def fill(c):
        return pltpu.make_async_copy(
            grad_ref.at[:, pl.ds(c * depth, depth)], og.at[c // 2, c % 2, t], fill_sem.at[c]
        )

    def wfill():
        return pltpu.make_async_copy(weight_ref, wfull.at[chip, core], wfill_sem)

    def go_right(p, s):
        at = og.at[behind(p // 2), p % 2, lax.rem(t - s + 1 + n, n)]
        return pltpu.make_async_remote_copy(
            at, at, rsend_sem.at[p, s - 1], rrecv_sem.at[p, s - 1],
            device_id=(d, lax.rem(t + 1, n)), device_id_type=MESH)

    def from_left(p, s):
        at = og.at[behind(p // 2), p % 2, lax.rem(t - s + n, n)]
        return pltpu.make_async_remote_copy(
            at, at, rsend_sem.at[p, s - 1], rrecv_sem.at[p, s - 1],
            device_id=(d, lax.rem(t + 1, n)), device_id_type=MESH)

    def go_left(p, s):
        at = og.at[behind(p // 2), p % 2, lax.rem(t + s - 1, n)]
        return pltpu.make_async_remote_copy(
            at, at, lsend_sem.at[p, s - 1], lrecv_sem.at[p, s - 1],
            device_id=(d, lax.rem(t - 1 + n, n)), device_id_type=MESH)

    def from_right(p, s):
        at = og.at[behind(p // 2), p % 2, lax.rem(t + s, n)]
        return pltpu.make_async_remote_copy(
            at, at, lsend_sem.at[p, s - 1], lrecv_sem.at[p, s - 1],
            device_id=(d, lax.rem(t - 1 + n, n)), device_id_type=MESH)

    def w_out(p):
        at = wfull.at[chip, core]
        return pltpu.make_async_remote_copy(
            at, at, wsend_sem.at[p], wrecv_sem.at[p],
            device_id=(ahead(p) * 2 + core, t), device_id_type=MESH)

    def w_in(p):
        at = wfull.at[behind(p), core]
        return pltpu.make_async_remote_copy(
            at, at, wsend_sem.at[p], wrecv_sem.at[p],
            device_id=(ahead(p) * 2 + core, t), device_id_type=MESH)

    def w_across(p):
        at = wfull.at[behind(p), core]
        return pltpu.make_async_remote_copy(
            at, at, wxsend_sem.at[p], wxrecv_sem.at[p], device_id=sibling, device_id_type=MESH)

    def w_from_sibling(p):
        at = wfull.at[behind(p), 1 - core]
        return pltpu.make_async_remote_copy(
            at, at, wxsend_sem.at[p], wxrecv_sem.at[p], device_id=sibling, device_id_type=MESH)

    def x_copy(p):
        return pltpu.make_async_remote_copy(
            xsend.at[p], xrecv.at[p], xsend_sem.at[p], xrecv_sem.at[p],
            device_id=sibling, device_id_type=MESH)

    def rs_copy(p):
        return pltpu.make_async_remote_copy(
            rs_send.at[p], rs_recv.at[p], rss_sem.at[p], rsr_sem.at[p],
            device_id=(behind(p) * 2 + core, t), device_id_type=MESH)

    def kv_copy(which):
        return pltpu.make_async_remote_copy(
            kv_send.at[which], kv_recv.at[which], kvs_sem.at[which], kvr_sem.at[which], device_id=partner, device_id_type=MESH)

    def send_own(p):
        @pl.when(has_right)
        def _():
            go_right(p, 1).start()

        @pl.when(has_left)
        def _():
            go_left(p, 1).start()

    for j in range(2 * nchip):
        fill(j).start()
    wfill().start()

    barrier = pltpu.get_barrier_semaphore()

    @pl.when(has_left)
    def _():
        pl.semaphore_signal(barrier, 1, device_id=(d, lax.rem(t - 1 + n, n)), device_id_type=MESH)

    @pl.when(has_right)
    def _():
        pl.semaphore_signal(barrier, 1, device_id=(d, lax.rem(t + 1, n)), device_id_type=MESH)

    pl.semaphore_signal(barrier, 1, device_id=sibling, device_id_type=MESH)
    for p in range(nchip - 1):
        pl.semaphore_signal(barrier, 1, device_id=(ahead(p) * 2 + core, t), device_id_type=MESH)
    inner = has_left & has_right

    @pl.when(inner)
    def _():
        pl.semaphore_wait(barrier, nchip + 2)

    @pl.when(jnp.logical_not(inner))
    def _():
        pl.semaphore_wait(barrier, nchip + 1)

    for j in range(2 * nchip):
        fill(j).wait()
    wfill().wait()
    for p in range(min(4, 2 * nchip)):
        send_own(p)
    for p in range(nchip - 1):
        w_out(p).start()
    w_across(nchip - 1).start()

    seg_col[...] = jnp.transpose(jnp.broadcast_to(seg_ref[...], (128, length)))
    rows = min(ROWS, length)
    blocks = length // rows

    def row_block(b):
        return pl.ds(pl.multiple_of(b * rows, rows), rows)

    def forward(b, carry):
        at = row_block(b)
        same = seg_col[at, :][:, :1] == seg_ref[...]
        row = lax.broadcasted_iota(jnp.int32, (rows, length), 0) + b * rows
        col = lax.broadcasted_iota(jnp.int32, (rows, length), 1)
        visible = same & (row >= col)
        for h in range(heads):
            cols = slice(h * HD, (h + 1) * HD)
            scores = dot(q_ref[at, cols], k_ref[...], 1, 1) * scale
            masked = jnp.where(visible, scores, -jnp.inf)
            raw = jnp.exp(masked - jnp.max(masked, axis=-1, keepdims=True))
            p_full = raw / jnp.sum(raw, axis=-1, keepdims=True)
            prob[h, at, :] = p_full
            attn[at, cols] = dot(p_full.astype(BF16), v_ref[...], 1, 0).astype(BF16)
        return carry

    lax.fori_loop(0, blocks, forward, 0)
    gsum[...] = jnp.zeros_like(gsum)

    def weight_term(p, which):
        block = og[behind(p), which].reshape(length, depth)
        return dot(block, attn[...], 0, 0).astype(BF16)

    def weight_terms(p):
        xsend[p] = weight_term(p, 1 - core)
        x_copy(p).start()
        part[p] = weight_term(p, core)

    def step(i, carry):
        @pl.when(i + 4 < 2 * nchip)
        def _():
            send_own(i + 4)

        done = i - n

        @pl.when((done >= 0) & (done % 2 == 0))
        def _():
            p = done // 2
            x_copy(p).wait_recv()
            rs_send[p] = (part[p].astype(F32) + xrecv[p].astype(F32)).astype(BF16)
            rs_copy(p).start()

        for s in range(1, n):
            p = i - (s - 1)
            live = (p >= 0) & (p < 2 * nchip)

            @pl.when(live & (t >= s))
            def _():
                from_left(p, s).wait_recv()

            @pl.when(live & (t + s < n))
            def _():
                from_right(p, s).wait_recv()

            if s < n - 1:
                @pl.when(live & (t >= s) & has_right)
                def _():
                    go_right(p, s + 1).start()

                @pl.when(live & (t + s < n) & has_left)
                def _():
                    go_left(p, s + 1).start()

        early = i - max(n - 3, 0)

        @pl.when((early >= 0) & (early < 2 * (nchip - 1)) & (early % 2 == 0))
        def _():
            w_in(early // 2).wait_recv()
            w_across(early // 2).start()

        now = i - (n - 2)

        @pl.when(now >= 0)
        def _():
            p, half = now // 2, now % 2

            @pl.when(half == 0)
            def _():
                w_from_sibling(p).wait_recv()

            j = behind(p)
            gsum[...] += dot(og[j, half].reshape(length, depth), wfull[j, half], 1, 0)

            @pl.when((half == 1) & (p < nchip - 1))
            def _():
                weight_terms(p)

        return carry

    lax.fori_loop(0, 2 * nchip + n - 2, step, 0)

    def backward_values(b, dv_sum):
        at = row_block(b)
        for h in range(heads):
            gh = gsum[at, h * HD:(h + 1) * HD].astype(BF16)
            dv_sum = dv_sum + dot(prob[h, at, :].astype(BF16), gh, 0, 0)
        return dv_sum

    def backward_keys(b, dk_sum):
        at = row_block(b)
        for h in range(heads):
            cols = slice(h * HD, (h + 1) * HD)
            gh = gsum[at, cols].astype(BF16)
            delta = jnp.sum(
                gh.astype(F32) * attn[at, cols].astype(F32), axis=-1, keepdims=True)
            gs = (prob[h, at, :] * (dot(gh, v_ref[...], 1, 1) - delta) * scale).astype(BF16)
            dk_sum = dk_sum + dot(gs, q_ref[at, cols], 0, 0)
            score_grad[h, at, :] = gs
        return dk_sum

    def backward_queries(b, carry):
        at = row_block(b)
        for h in range(heads):
            dq_ref[at, h * HD:(h + 1) * HD] = dot(
                score_grad[h, at, :], k_ref[...], 1, 0).astype(BF16)
        return carry

    def over_blocks(body, init):
        return body(0, init) if blocks == 1 else lax.fori_loop(0, blocks, body, init)

    zero = jnp.zeros((length, HD), F32)
    dv_sum = over_blocks(backward_values, zero)
    kv_send[1] = dv_sum.astype(BF16)
    kv_copy(1).start()
    dk_sum = over_blocks(backward_keys, zero)
    kv_send[0] = dk_sum.astype(BF16)
    kv_copy(0).start()
    over_blocks(backward_queries, 0)
    last = nchip - 1
    weight_terms(last)
    kv_copy(1).wait_recv()
    kv_copy(0).wait_recv()
    dk_ref[...] = (dk_sum + kv_recv[0].astype(F32)).astype(BF16)
    dv_ref[...] = (dv_sum + kv_recv[1].astype(F32)).astype(BF16)

    x_copy(last).wait_recv()
    total = part[last].astype(F32) + xrecv[last].astype(F32)
    for p in range(nchip - 1):
        rs_copy(p).wait_recv()
        total = total + rs_recv[p].astype(F32)
    dw_ref[...] = total * (1.0 / (2 * nchip))

    kv_copy(1).wait_send()
    kv_copy(0).wait_send()

    def drain(p, carry):
        x_copy(p).wait_send()
        w_across(p).wait_send()

        @pl.when(p < nchip - 1)
        def _():
            w_out(p).wait_send()
            rs_copy(p).wait_send()

        return carry

    def drain_line(p, carry):
        for s in range(1, n):
            @pl.when(has_right & (t >= s - 1))
            def _():
                go_right(p, s).wait_send()

            @pl.when(has_left & (t + s - 1 < n))
            def _():
                go_left(p, s).wait_send()

        return carry

    lax.fori_loop(0, 2 * nchip, drain_line, 0)
    lax.fori_loop(0, nchip, drain, 0)


def hand_out(*refs):
    for source, result in zip(refs[:4], refs[4:]):
        result[...] = source[...]


def local(nchip, n, out_grad, out_weight, queries, keys, values, segment_ids):
    grad, q, k, v = out_grad[0], queries[0], keys[0], values[0]
    rows, model = grad.shape
    depth, width = out_weight.shape
    length = q.shape[0]
    heads = width // HD
    vmem = pl.BlockSpec(memory_space=pltpu.VMEM)
    hbm = pl.BlockSpec(memory_space=pl.ANY)
    dma = pltpu.SemaphoreType.DMA
    most = max(nchip - 1, 1)
    results = pl.pallas_call(
        functools.partial(kernel, nchip, n),
        out_shape=(
            jax.ShapeDtypeStruct((length, width), BF16),
            jax.ShapeDtypeStruct((length, HD), BF16),
            jax.ShapeDtypeStruct((length, HD), BF16),
            jax.ShapeDtypeStruct((depth, width), F32),
        ),
        in_specs=[hbm, hbm, vmem, vmem, vmem, vmem],
        out_specs=(vmem, vmem, vmem, vmem),
        scratch_shapes=[
            pltpu.VMEM((nchip, 2, n, rows, depth), BF16),
            pltpu.VMEM((nchip, 2, depth, width), BF16),
            pltpu.VMEM((heads, length, length), F32),
            pltpu.VMEM((heads, length, length), BF16),
            pltpu.VMEM((length, 128), jnp.int32),
            pltpu.VMEM((length, width), BF16),
            pltpu.VMEM((length, width), F32),
            pltpu.VMEM((2, length, HD), BF16),
            pltpu.VMEM((2, length, HD), BF16),
            pltpu.VMEM((nchip, depth, width), BF16),
            pltpu.VMEM((nchip, depth, width), BF16),
            pltpu.VMEM((nchip, depth, width), BF16),
            pltpu.VMEM((most, depth, width), BF16),
            pltpu.VMEM((most, depth, width), BF16),
            dma((2 * nchip,)), dma,
            dma((2 * nchip, n - 1)), dma((2 * nchip, n - 1)),
            dma((2 * nchip, n - 1)), dma((2 * nchip, n - 1)),
            dma((most,)), dma((most,)), dma((nchip,)), dma((nchip,)),
            dma((nchip,)), dma((nchip,)), dma((most,)), dma((most,)),
            dma((2,)), dma((2,)),
        ],
        compiler_params=pltpu.CompilerParams(
            collective_id=0, has_side_effects=True, vmem_limit_bytes=56 << 20),
        cost_estimate=pl.CostEstimate(
            flops=4 * length * model * width, bytes_accessed=8 << 20, transcendentals=0),
    )(grad, out_weight, q, k, v, segment_ids)
    dq, dk, dv, dw = pl.pallas_call(
        hand_out,
        out_shape=tuple(jax.ShapeDtypeStruct(r.shape, r.dtype) for r in results),
        in_specs=[vmem] * 4,
        out_specs=(vmem,) * 4,
    )(*results)
    return dq[None], dk[None], dv[None], dw


def solution(mesh):
    in_specs = (
        P("dp", "tensor", None),
        P("dp", "tensor"),
        P("dp", None, "tensor"),
        P("dp", None, "tensor"),
        P("dp", None, "tensor"),
        P("dp", None),
    )
    out_specs = (
        P("dp", None, "tensor"),
        P("dp", None, "tensor"),
        P("dp", None, "tensor"),
        P("dp", "tensor"),
    )
    body = functools.partial(local, mesh.shape["dp"] // 2, mesh.shape["tensor"])
    return jax.shard_map(body, mesh=mesh, in_specs=in_specs, out_specs=out_specs, check_vma=False)
```
